32 devices in a mesh: row: 4 (over x, core), col: 8 (over z, y).
Axes of the slice: x: 2, y: 2, z: 4, core: 2. Of those that a mesh axis runs over, the one named last changes fastest.
Arguments:
- tokens: bfloat16 [512, 6144], P('row', 'col'), may hold values from -6 to 6
- out_grad: bfloat16 [512, 6144], P('row', 'col'), may hold values from -6 to 6
- pre_act: bfloat16 [512, 24576], P('col', 'row'), may hold values from -6 to 6
- w_in: bfloat16 [6144, 24576], P('col', 'row'), may hold values from -0.078125 to 0.078125
- w_out: bfloat16 [24576, 6144], P('row', 'col'), may hold values from -0.0390625 to 0.0390625
Outputs:
- grad_tokens: bfloat16 [512, 6144], P('row', 'col')
- grad_w_in: bfloat16 [6144, 24576], P('col', 'row')
- grad_w_out: bfloat16 [24576, 6144], P('row', 'col')
The draws below stay inside these ranges and needn't reach their ends.
All inputs are finite; a program needn't handle non-finite values.
Results may differ from the reference program's by a relative error of at most 0.03.
Values may be sent and summed in bfloat16 or wider, within the bound.
A program may use at most 128 MiB of HBM per device.

```python
import math
import jax
import jax.numpy as jnp
from jax import lax

D = 6144
FF = 24576
TOKENS = 512
N_ROW = 4
N_COL = 8


def levels(rng, shape, shards, low, high):
    def one(position, parts):
        draws = jax.random.uniform(jax.random.fold_in(jax.random.fold_in(rng, 6), position), (parts,), jnp.float32, low / len(shards), high / len(shards))
        return jnp.repeat(jnp.exp(draws), shape[position] // parts).reshape((-1,) + (1,) * (len(shape) - position - 1))

    gain = one(*shards[0])
    for cut in shards[1:]:
        gain = gain * one(*cut)
    return gain


def scatter_about(rng, shape, deviation, limit, pieces=(), dtype=jnp.bfloat16):
    loudness = levels(rng, shape, pieces, -0.22, 0.18) if pieces else 1.0
    result = jax.random.normal(rng, shape, jnp.float32) * deviation * loudness
    return jnp.minimum(jnp.maximum(result, -limit), limit).astype(dtype)


def setup_inputs(seed: int = 0) -> dict:
    keys = jax.random.split(jax.random.key(seed), 6)
    return {
        "tokens": scatter_about(keys[0], (TOKENS, D), 1.0, 6.0, ((0, 4), (1, 8))),
        "out_grad": scatter_about(keys[1], (TOKENS, D), 1.0, 6.0, ((0, 4), (1, 8))),
        "pre_act": scatter_about(keys[2], (TOKENS, FF), 1.5, 6.0, ((0, 8), (1, 4))),
        "w_in": scatter_about(keys[3], (D, FF), D ** -0.5, 0.078125, ((0, 8), (1, 4))),
        "w_out": scatter_about(keys[4], (FF, D), FF ** -0.5, 0.0390625, ((0, 4), (1, 8))),
    }


gelu_coef = math.sqrt(2.0 / math.pi)
cubic_coef = 0.044715

def gelu_parts(pre_values):
    pre_f32 = pre_values.astype(jnp.float32)
    tangent = jnp.tanh(gelu_coef * (pre_f32 + cubic_coef * pre_f32 * pre_f32 * pre_f32))
    activated = 0.5 * pre_f32 * (1.0 + tangent)
    slopes = 0.5 * (1.0 + tangent) + 0.5 * pre_f32 * (1.0 - tangent * tangent) * gelu_coef * (1.0 + 3.0 * cubic_coef * pre_f32 * pre_f32)
    return (activated, slopes)

def contract(left_side, right_side, left_dim, right_dim):
    return lax.dot_general(left_side, right_side, (((left_dim,), (right_dim,)), ((), ())), preferred_element_type=jnp.float32)

def reference(tokens, out_grad, pre_act, w_in, w_out):
    activated, slopes = gelu_parts(pre_act)
    hidden = activated.astype(jnp.bfloat16)
    block_width = D // N_COL
    hidden_grad = jnp.zeros((TOKENS, FF), jnp.float32)
    for block in range(N_COL):
        lower = block * block_width
        partial_term = contract(out_grad[:, lower:lower + block_width], w_out[:, lower:lower + block_width], 1, 1)
        rounded = lax.optimization_barrier(partial_term.astype(jnp.bfloat16))
        hidden_grad = hidden_grad + rounded.astype(jnp.float32)
    pre_grad = (hidden_grad * slopes).astype(jnp.bfloat16)
    grad_scale = float(TOKENS) ** (-0.5)
    grad_w_out = (contract(hidden, out_grad, 0, 0) * grad_scale).astype(jnp.bfloat16)
    grad_w_in = (contract(tokens, pre_grad, 0, 0) * grad_scale).astype(jnp.bfloat16)
    unit_width = FF // N_ROW
    token_total = jnp.zeros((TOKENS, D), jnp.float32)
    for block in range(N_ROW):
        lower = block * unit_width
        partial_term = contract(pre_grad[:, lower:lower + unit_width], w_in[:, lower:lower + unit_width], 1, 1)
        rounded = lax.optimization_barrier(partial_term.astype(jnp.bfloat16))
        token_total = token_total + rounded.astype(jnp.float32)
    grad_tokens = token_total.astype(jnp.bfloat16)
    return (grad_tokens, grad_w_in, grad_w_out)
```

```python
import functools
import math

import jax
import jax.numpy as jnp
from jax import lax
from jax.experimental import pallas as pl
from jax.experimental.pallas import tpu as pltpu
from jax.sharding import PartitionSpec as P

gelu_coef = math.sqrt(2.0 / math.pi)
cubic_coef = 0.044715
MESH = pl.DeviceIdType.MESH
CHUNKS = 4


def gelu_parts(pre_f32):
    tangent = jnp.tanh(gelu_coef * (pre_f32 + cubic_coef * pre_f32 * pre_f32 * pre_f32))
    activated = 0.5 * pre_f32 * (1.0 + tangent)
    slopes = 0.5 * (1.0 + tangent) + 0.5 * pre_f32 * (1.0 - tangent * tangent) * gelu_coef * (
        1.0 + 3.0 * cubic_coef * pre_f32 * pre_f32
    )
    return (activated, slopes)


def contract(left_side, right_side, left_dim, right_dim):
    return lax.dot_general(
        left_side,
        right_side,
        (((left_dim,), (right_dim,)), ((), ())),
        preferred_element_type=jnp.float32,
    )


def exchange_kernel(
    n_row, n_col,
    tok_ref, grad_ref, pre_ref, w_ref,
    tok_all, grad_all, act_all, pg_all,
    g_v, w_v, h_v, a_v, p_v, in_v, slope_v,
    w_sem, own_sem, out_sem,
    g_send, g_recv, x_send, x_recv,
    h_send, h_recv, a_send, a_recv, p_send, p_recv,
):
    rows = grad_ref.shape[0]
    share = pre_ref.shape[0]
    width = w_v.shape[1]
    tile = 256 if width % 256 == 0 else 128
    last = n_col - 2
    row = lax.axis_index("row")
    col = lax.axis_index("col")
    odd = col % 2
    pos = (1 - odd) * (col // 2) + odd * (n_col - 1 - col // 2)

    def col_at(place):
        place = (place + 2 * n_col) % n_col
        back = place // (n_col // 2)
        return (1 - back) * (2 * place) + back * (2 * (n_col - 1 - place) + 1)

    def row_slice(index, size):
        return pl.ds(pl.multiple_of(index * size, size), size)

    def sign(q):
        return 1 if q % 2 == 0 else -1

    def ring(q, src, dst, send_sem, recv_sem):
        return pltpu.make_async_remote_copy(
            src_ref=src, dst_ref=dst, send_sem=send_sem, recv_sem=recv_sem,
            device_id=(row, col_at(pos + sign(q))), device_id_type=MESH,
        )

    def h_copy(q, step):
        return ring(q, in_v.at[q, step], in_v.at[q, step + 1], h_send.at[q, step + 1], h_recv.at[q, step + 1])

    def h_arrival(q, step):
        block = in_v.at[q, step]
        return ring(q, block, block, h_send.at[q, step], h_recv.at[q, step])

    def h_first(q):
        block = h_v.at[q, row_slice(col_at(pos - sign(q)), share)]
        return ring(q, block, in_v.at[q, 0], h_send.at[q, 0], h_recv.at[q, 0])

    def gather_copy(buf, send_sem, recv_sem, q, step):
        block = buf.at[q, row_slice(col_at(pos - sign(q) * step), share)]
        return ring(q, block, block, send_sem.at[q, step], recv_sem.at[q, step])

    def gather_arrival(buf, send_sem, recv_sem, q, step):
        block = buf.at[q, row_slice(col_at(pos - sign(q) * (step + 1)), share)]
        return ring(q, block, block, send_sem.at[q, step], recv_sem.at[q, step])

    a_ring = (a_v, a_send, a_recv)
    p_ring = (p_v, p_send, p_recv)

    w_loads = [
        pltpu.make_async_copy(w_ref.at[pl.ds(q * width, width)], w_v.at[q], w_sem.at[q])
        for q in range(CHUNKS)
    ]
    for load in w_loads:
        load.start()

    barrier = pltpu.get_barrier_semaphore()
    for k in range(1, n_row):
        pl.semaphore_signal(barrier, inc=1, device_id=((row + k) % n_row, col), device_id_type=MESH)
    for side in (1, -1):
        pl.semaphore_signal(barrier, inc=1, device_id=(row, col_at(pos + side)), device_id_type=MESH)
    pl.semaphore_wait(barrier, n_row + 1)

    def row_copy(src, dst, send_sem, recv_sem, k, owner):
        return pltpu.make_async_remote_copy(
            src_ref=src, dst_ref=dst.at[row_slice(owner, rows)],
            send_sem=send_sem.at[k - 1], recv_sem=recv_sem.at[k - 1],
            device_id=((row + k) % n_row, col), device_id_type=MESH,
        )

    for k in range(1, n_row):
        row_copy(grad_ref, g_v, g_send, g_recv, k, row).start()
    g_v[row_slice(row, rows), :] = grad_ref[...]

    for q in range(CHUNKS):
        @pl.loop(0, width // tile)
        def _(j, q=q):
            lanes = pl.ds(pl.multiple_of(j * tile, tile), tile)
            source = pl.ds(pl.multiple_of(q * width + j * tile, 128), tile)
            activated, slopes = gelu_parts(pre_ref[:, source].astype(jnp.float32))
            a_v[q, row_slice(col, share), lanes] = activated.astype(jnp.bfloat16)
            slope_v[q, :, lanes] = slopes

        gather_copy(*a_ring, q, 0).start()

    for k in range(1, n_row):
        row_copy(grad_ref, g_v, g_send, g_recv, k, (row + n_row - k) % n_row).wait_recv()

    for q in range(CHUNKS):
        w_loads[q].wait()

        @pl.loop(0, width // tile)
        def _(j, q=q):
            lanes = pl.ds(pl.multiple_of(j * tile, tile), tile)
            h_v[q, :, lanes] = contract(g_v[...], w_v[q, lanes, :], 1, 1).astype(jnp.bfloat16)

        h_first(q).start()

    for k in range(1, n_row):
        row_copy(tok_ref, tok_all, x_send, x_recv, k, row).start()
    own_tokens = pltpu.make_async_copy(tok_ref, tok_all.at[row_slice(row, rows)], own_sem.at[0])
    own_tokens.start()
    grad_out = pltpu.make_async_copy(g_v, grad_all, own_sem.at[1])
    grad_out.start()

    @pl.loop(0, last)
    def _(step):
        for q in range(CHUNKS):
            h_arrival(q, step).wait_recv()
            own = h_v[q, row_slice(col_at(pos - sign(q) * (step + 2)), share), :]
            total = in_v[q, step].astype(jnp.float32) + own.astype(jnp.float32)
            in_v[q, step] = total.astype(jnp.bfloat16)
            h_copy(q, step).start()
            gather_arrival(*a_ring, q, step).wait_recv()
            gather_copy(*a_ring, q, step + 1).start()

    for q in range(CHUNKS):
        h_arrival(q, last).wait_recv()
        mine = row_slice(col, share)
        total = in_v[q, last].astype(jnp.float32) + h_v[q, mine, :].astype(jnp.float32)
        p_v[q, mine, :] = (total * slope_v[q]).astype(jnp.bfloat16)
        gather_copy(*p_ring, q, 0).start()

    def write_out(buf, out, q, which):
        return pltpu.make_async_copy(
            buf.at[q], out.at[:, pl.ds(q * width, width)], out_sem.at[which, q]
        )

    for q in range(CHUNKS):
        gather_arrival(*a_ring, q, last).wait_recv()
        write_out(a_v, act_all, q, 0).start()

    @pl.loop(0, last)
    def _(step):
        for q in range(CHUNKS):
            gather_arrival(*p_ring, q, step).wait_recv()
            gather_copy(*p_ring, q, step + 1).start()

    for q in range(CHUNKS):
        gather_arrival(*p_ring, q, last).wait_recv()
        write_out(p_v, pg_all, q, 1).start()

    for k in range(1, n_row):
        row_copy(grad_ref, g_v, g_send, g_recv, k, row).wait_send()
        row_copy(tok_ref, tok_all, x_send, x_recv, k, row).wait_send()
        row_copy(tok_ref, tok_all, x_send, x_recv, k, (row + n_row - k) % n_row).wait_recv()
    own_tokens.wait()
    grad_out.wait()

    for q in range(CHUNKS):
        h_first(q).wait_send()

        @pl.loop(0, last)
        def _(step, q=q):
            h_copy(q, step).wait_send()

        @pl.loop(0, last + 1)
        def _(step, q=q):
            gather_copy(*a_ring, q, step).wait_send()
            gather_copy(*p_ring, q, step).wait_send()

        write_out(a_v, act_all, q, 0).wait()
        write_out(p_v, pg_all, q, 1).wait()


def body(n_row, n_col, tokens, out_grad, pre_act, w_in, w_out):
    rows, depth = tokens.shape
    share, units = pre_act.shape
    total = rows * n_row
    width = units // CHUNKS
    half = jnp.bfloat16
    dma = pltpu.SemaphoreType.DMA
    ring_sem = dma((CHUNKS, n_col - 1))
    row_sem = dma((n_row - 1,))
    vmem = pl.BlockSpec(memory_space=pltpu.VMEM)
    anywhere = pl.BlockSpec(memory_space=pl.ANY)
    tok_all, grad_all, hid_all, pregrad_all = pl.pallas_call(
        functools.partial(exchange_kernel, n_row, n_col),
        out_shape=(
            jax.ShapeDtypeStruct((total, depth), half),
            jax.ShapeDtypeStruct((total, depth), half),
            jax.ShapeDtypeStruct((total, units), half),
            jax.ShapeDtypeStruct((total, units), half),
        ),
        in_specs=[vmem, vmem, vmem, anywhere],
        out_specs=(anywhere,) * 4,
        scratch_shapes=[
            pltpu.VMEM((total, depth), half),
            pltpu.VMEM((CHUNKS, width, depth), half),
            pltpu.VMEM((CHUNKS, total, width), half),
            pltpu.VMEM((CHUNKS, total, width), half),
            pltpu.VMEM((CHUNKS, total, width), half),
            pltpu.VMEM((CHUNKS, n_col - 1, share, width), half),
            pltpu.VMEM((CHUNKS, share, width), jnp.float32),
            dma((CHUNKS,)), dma((2,)), dma((2, CHUNKS)),
            row_sem, row_sem, row_sem, row_sem,
            ring_sem, ring_sem, ring_sem, ring_sem, ring_sem, ring_sem,
        ],
        compiler_params=pltpu.CompilerParams(
            collective_id=0, has_side_effects=True, vmem_limit_bytes=56 * 2**20
        ),
        cost_estimate=pl.CostEstimate(
            flops=2 * total * depth * units, bytes_accessed=40 * 2**20, transcendentals=share * units
        ),
        name="exchange",
    )(tokens, out_grad, pre_act, w_out)
    grad_scale = float(total) ** (-0.5)
    grad_tokens = lax.psum_scatter(
        contract(pregrad_all, w_in, 1, 1).astype(half), "row", scatter_dimension=0, tiled=True
    )
    grad_w_out = (contract(hid_all, grad_all, 0, 0) * grad_scale).astype(half)
    grad_w_in = (contract(tok_all, pregrad_all, 0, 0) * grad_scale).astype(half)
    return (grad_tokens, grad_w_in, grad_w_out)


def solution(mesh):
    in_specs = (P("row", "col"), P("row", "col"), P("col", "row"), P("col", "row"), P("row", "col"))
    out_specs = (P("row", "col"), P("col", "row"), P("row", "col"))
    sizes = (mesh.shape["row"], mesh.shape["col"])
    return jax.shard_map(
        functools.partial(body, *sizes), mesh=mesh, in_specs=in_specs, out_specs=out_specs, check_vma=False
    )
```

```python
import functools
import math

import jax
import jax.numpy as jnp
from jax import lax
from jax.experimental import pallas as pl
from jax.experimental.pallas import tpu as pltpu
from jax.sharding import PartitionSpec as P

gelu_coef = math.sqrt(2.0 / math.pi)
cubic_coef = 0.044715
MESH = pl.DeviceIdType.MESH
CHUNKS = 4


def gelu_parts(pre_f32):
    tangent = jnp.tanh(gelu_coef * (pre_f32 + cubic_coef * pre_f32 * pre_f32 * pre_f32))
    activated = 0.5 * pre_f32 * (1.0 + tangent)
    slopes = 0.5 * (1.0 + tangent) + 0.5 * pre_f32 * (1.0 - tangent * tangent) * gelu_coef * (
        1.0 + 3.0 * cubic_coef * pre_f32 * pre_f32
    )
    return (activated, slopes)


def contract(left_side, right_side, left_dim, right_dim):
    return lax.dot_general(
        left_side,
        right_side,
        (((left_dim,), (right_dim,)), ((), ())),
        preferred_element_type=jnp.float32,
    )


def exchange_kernel(
    n_row, n_col,
    tok_ref, grad_ref, pre_ref, w_ref, w_in_ref,
    tok_all, grad_all, act_all, pg_all, gt_ref,
    g_v, w_v, h_v, a_v, p_v, in_v, slope_v, wi_v, part_v, terms_v,
    w_sem, wi_sem, own_sem, out_sem, t_send, t_recv,
    g_send, g_recv, x_send, x_recv,
    h_send, h_recv, a_send, a_recv, p_send, p_recv,
):
    rows = grad_ref.shape[0]
    share = pre_ref.shape[0]
    width = w_v.shape[1]
    tile = 256 if width % 256 == 0 else 128
    last = n_col - 2
    row = lax.axis_index("row")
    col = lax.axis_index("col")
    odd = col % 2
    pos = (1 - odd) * (col // 2) + odd * (n_col - 1 - col // 2)

    def col_at(place):
        place = (place + 2 * n_col) % n_col
        back = place // (n_col // 2)
        return (1 - back) * (2 * place) + back * (2 * (n_col - 1 - place) + 1)

    def row_slice(index, size):
        return pl.ds(pl.multiple_of(index * size, size), size)

    def sign(q):
        return 1 if q % 2 == 0 else -1

    def ring(q, src, dst, send_sem, recv_sem):
        return pltpu.make_async_remote_copy(
            src_ref=src, dst_ref=dst, send_sem=send_sem, recv_sem=recv_sem,
            device_id=(row, col_at(pos + sign(q))), device_id_type=MESH,
        )

    def h_copy(q, step):
        return ring(q, in_v.at[q, step], in_v.at[q, step + 1], h_send.at[q, step + 1], h_recv.at[q, step + 1])

    def h_arrival(q, step):
        block = in_v.at[q, step]
        return ring(q, block, block, h_send.at[q, step], h_recv.at[q, step])

    def h_first(q):
        block = h_v.at[q, row_slice(col_at(pos - sign(q)), share)]
        return ring(q, block, in_v.at[q, 0], h_send.at[q, 0], h_recv.at[q, 0])

    def gather_copy(buf, send_sem, recv_sem, q, step):
        block = buf.at[q, row_slice(col_at(pos - sign(q) * step), share)]
        return ring(q, block, block, send_sem.at[q, step], recv_sem.at[q, step])

    def gather_arrival(buf, send_sem, recv_sem, q, step):
        block = buf.at[q, row_slice(col_at(pos - sign(q) * (step + 1)), share)]
        return ring(q, block, block, send_sem.at[q, step], recv_sem.at[q, step])

    a_ring = (a_v, a_send, a_recv)
    p_ring = (p_v, p_send, p_recv)

    w_loads = [
        pltpu.make_async_copy(w_ref.at[pl.ds(q * width, width)], w_v.at[q], w_sem.at[q])
        for q in range(CHUNKS)
    ]
    for load in w_loads:
        load.start()

    barrier = pltpu.get_barrier_semaphore()
    for k in range(1, n_row):
        pl.semaphore_signal(barrier, inc=1, device_id=((row + k) % n_row, col), device_id_type=MESH)
    for side in (1, -1):
        pl.semaphore_signal(barrier, inc=1, device_id=(row, col_at(pos + side)), device_id_type=MESH)
    pl.semaphore_wait(barrier, n_row + 1)

    def row_copy(src, dst, send_sem, recv_sem, k, owner):
        return pltpu.make_async_remote_copy(
            src_ref=src, dst_ref=dst.at[row_slice(owner, rows)],
            send_sem=send_sem.at[k - 1], recv_sem=recv_sem.at[k - 1],
            device_id=((row + k) % n_row, col), device_id_type=MESH,
        )

    pairs = n_row // 2
    sibling = row + 1 - 2 * (row % 2)

    def peer(m):
        return (row + 2 * m) % n_row

    def source_of(m):
        return (row + n_row - 2 * m) % n_row

    def grad_copy(index, src, owner, target):
        return pltpu.make_async_remote_copy(
            src_ref=src, dst_ref=g_v.at[row_slice(owner, rows)],
            send_sem=g_send.at[index], recv_sem=g_recv.at[index],
            device_id=(target, col), device_id_type=MESH,
        )

    def grad_arrival(index, owner):
        return grad_copy(index, grad_ref, owner, sibling)

    def grad_relay(m):
        owner = source_of(m)
        return grad_copy(pairs - 1 + m, g_v.at[row_slice(owner, rows)], owner, sibling)

    for m in range(1, pairs):
        grad_copy(m, grad_ref, row, peer(m)).start()
    grad_copy(0, grad_ref, row, sibling).start()
    g_v[row_slice(row, rows), :] = grad_ref[...]

    def forward_activated(step):
        for q in range(CHUNKS):
            gather_arrival(*a_ring, q, step).wait_recv()
            gather_copy(*a_ring, q, step + 1).start()

    for q in range(CHUNKS):
        @pl.loop(0, width // tile)
        def _(j, q=q):
            lanes = pl.ds(pl.multiple_of(j * tile, tile), tile)
            source = pl.ds(pl.multiple_of(q * width + j * tile, 128), tile)
            activated, slopes = gelu_parts(pre_ref[:, source].astype(jnp.float32))
            a_v[q, row_slice(col, share), lanes] = activated.astype(jnp.bfloat16)
            slope_v[q, :, lanes] = slopes

        gather_copy(*a_ring, q, 0).start()
        if q == 1:
            for m in range(1, pairs):
                grad_arrival(m, source_of(m)).wait_recv()
                grad_relay(m).start()

    grad_arrival(0, sibling).wait_recv()
    for m in range(1, pairs):
        grad_arrival(pairs - 1 + m, (sibling + n_row - 2 * m) % n_row).wait_recv()

    for q in range(CHUNKS):
        w_loads[q].wait()

        @pl.loop(0, width // tile)
        def _(j, q=q):
            lanes = pl.ds(pl.multiple_of(j * tile, tile), tile)
            h_v[q, :, lanes] = contract(g_v[...], w_v[q, lanes, :], 1, 1).astype(jnp.bfloat16)

        h_first(q).start()
        if q % 2 == 1:
            forward_activated(q // 2)

    wi_loads = [
        pltpu.make_async_copy(w_in_ref.at[:, pl.ds(q * width, width)], wi_v.at[q], wi_sem.at[q])
        for q in range(CHUNKS)
    ]
    for load in wi_loads:
        load.start()

    for k in range(1, n_row):
        row_copy(tok_ref, tok_all, x_send, x_recv, k, row).start()
    own_tokens = pltpu.make_async_copy(tok_ref, tok_all.at[row_slice(row, rows)], own_sem.at[0])
    own_tokens.start()
    grad_out = pltpu.make_async_copy(g_v, grad_all, own_sem.at[1])
    grad_out.start()

    def add_and_pass(q, step):
        h_arrival(q, step).wait_recv()
        own = h_v[q, row_slice(col_at(pos - sign(q) * (step + 2)), share), :]
        total = in_v[q, step].astype(jnp.float32) + own.astype(jnp.float32)
        in_v[q, step] = total.astype(jnp.bfloat16)
        h_copy(q, step).start()

    ahead = CHUNKS // 2

    @pl.loop(0, last - ahead)
    def _(step):
        for q in range(CHUNKS):
            add_and_pass(q, step)
            gather_arrival(*a_ring, q, step + ahead).wait_recv()
            gather_copy(*a_ring, q, step + ahead + 1).start()

    @pl.loop(last - ahead, last)
    def _(step):
        for q in range(CHUNKS):
            add_and_pass(q, step)

    for q in range(CHUNKS):
        h_arrival(q, last).wait_recv()
        mine = row_slice(col, share)
        total = in_v[q, last].astype(jnp.float32) + h_v[q, mine, :].astype(jnp.float32)
        p_v[q, mine, :] = (total * slope_v[q]).astype(jnp.bfloat16)
        gather_copy(*p_ring, q, 0).start()

    def write_out(buf, out, q, which):
        return pltpu.make_async_copy(
            buf.at[q], out.at[:, pl.ds(q * width, width)], out_sem.at[which, q]
        )

    for q in range(CHUNKS):
        gather_arrival(*a_ring, q, last).wait_recv()
        write_out(a_v, act_all, q, 0).start()

    @pl.loop(0, last)
    def _(step):
        for q in range(CHUNKS):
            gather_arrival(*p_ring, q, step).wait_recv()
            gather_copy(*p_ring, q, step + 1).start()

    for q in range(CHUNKS):
        gather_arrival(*p_ring, q, last).wait_recv()
        write_out(p_v, pg_all, q, 1).start()
        wi_loads[q].wait()

    def term_copy(j, k):
        target = (row + k) % n_row
        return pltpu.make_async_remote_copy(
            src_ref=part_v.at[j, row_slice(target, rows)], dst_ref=terms_v.at[j, k - 1],
            send_sem=t_send.at[j, k - 1], recv_sem=t_recv.at[j, k - 1],
            device_id=(target, col), device_id_type=MESH,
        )

    slabs, slab = part_v.shape[0], part_v.shape[2]
    for j in range(slabs):
        lines = pl.ds(j * slab, slab)
        total = contract(p_v[0], wi_v[0, lines, :], 1, 1)
        for q in range(1, CHUNKS):
            total = total + contract(p_v[q], wi_v[q, lines, :], 1, 1)
        part_v[j] = total.astype(jnp.bfloat16)
        for k in range(1, n_row):
            term_copy(j, k).start()

    for j in range(slabs):
        total = part_v[j, row_slice(row, rows), :].astype(jnp.float32)
        for k in range(1, n_row):
            term_copy(j, k).wait_recv()
            total = total + terms_v[j, k - 1].astype(jnp.float32)
        gt_ref[:, pl.ds(j * slab, slab)] = total.astype(jnp.bfloat16)

    for j in range(slabs):
        for k in range(1, n_row):
            term_copy(j, k).wait_send()
    grad_copy(0, grad_ref, row, sibling).wait_send()
    for m in range(1, pairs):
        grad_copy(m, grad_ref, row, peer(m)).wait_send()
        grad_relay(m).wait_send()
    for k in range(1, n_row):
        row_copy(tok_ref, tok_all, x_send, x_recv, k, row).wait_send()
        row_copy(tok_ref, tok_all, x_send, x_recv, k, (row + n_row - k) % n_row).wait_recv()
    own_tokens.wait()
    grad_out.wait()

    for q in range(CHUNKS):
        h_first(q).wait_send()

        @pl.loop(0, last)
        def _(step, q=q):
            h_copy(q, step).wait_send()

        @pl.loop(0, last + 1)
        def _(step, q=q):
            gather_copy(*a_ring, q, step).wait_send()
            gather_copy(*p_ring, q, step).wait_send()

        write_out(a_v, act_all, q, 0).wait()
        write_out(p_v, pg_all, q, 1).wait()


def body(n_row, n_col, tokens, out_grad, pre_act, w_in, w_out):
    rows, depth = tokens.shape
    share, units = pre_act.shape
    total = rows * n_row
    width = units // CHUNKS
    slab = 256 if depth % 256 == 0 else 128
    half = jnp.bfloat16
    dma = pltpu.SemaphoreType.DMA
    ring_sem = dma((CHUNKS, n_col - 1))
    row_sem = dma((n_row - 1,))
    vmem = pl.BlockSpec(memory_space=pltpu.VMEM)
    anywhere = pl.BlockSpec(memory_space=pl.ANY)
    tok_all, grad_all, hid_all, pregrad_all, grad_tokens = pl.pallas_call(
        functools.partial(exchange_kernel, n_row, n_col),
        out_shape=(
            jax.ShapeDtypeStruct((total, depth), half),
            jax.ShapeDtypeStruct((total, depth), half),
            jax.ShapeDtypeStruct((total, units), half),
            jax.ShapeDtypeStruct((total, units), half),
            jax.ShapeDtypeStruct((rows, depth), half),
        ),
        in_specs=[vmem, vmem, vmem, anywhere, anywhere],
        out_specs=(anywhere,) * 4 + (vmem,),
        scratch_shapes=[
            pltpu.VMEM((total, depth), half),
            pltpu.VMEM((CHUNKS, width, depth), half),
            pltpu.VMEM((CHUNKS, total, width), half),
            pltpu.VMEM((CHUNKS, total, width), half),
            pltpu.VMEM((CHUNKS, total, width), half),
            pltpu.VMEM((CHUNKS, n_col - 1, share, width), half),
            pltpu.VMEM((CHUNKS, share, width), jnp.float32),
            pltpu.VMEM((CHUNKS, depth, width), half),
            pltpu.VMEM((depth // slab, total, slab), half),
            pltpu.VMEM((depth // slab, n_row - 1, rows, slab), half),
            dma((CHUNKS,)), dma((CHUNKS,)), dma((2,)), dma((2, CHUNKS)),
            dma((depth // slab, n_row - 1)), dma((depth // slab, n_row - 1)),
            row_sem, row_sem, row_sem, row_sem,
            ring_sem, ring_sem, ring_sem, ring_sem, ring_sem, ring_sem,
        ],
        compiler_params=pltpu.CompilerParams(
            collective_id=0, has_side_effects=True, vmem_limit_bytes=58 * 2**20
        ),
        cost_estimate=pl.CostEstimate(
            flops=2 * total * depth * units, bytes_accessed=40 * 2**20, transcendentals=share * units
        ),
        name="exchange",
    )(tokens, out_grad, pre_act, w_out, w_in)
    grad_scale = float(total) ** (-0.5)
    grad_w_out = (contract(hid_all, grad_all, 0, 0) * grad_scale).astype(half)
    grad_w_in = (contract(tok_all, pregrad_all, 0, 0) * grad_scale).astype(half)
    return (grad_tokens, grad_w_in, grad_w_out)


def solution(mesh):
    in_specs = (P("row", "col"), P("row", "col"), P("col", "row"), P("col", "row"), P("row", "col"))
    out_specs = (P("row", "col"), P("col", "row"), P("row", "col"))
    sizes = (mesh.shape["row"], mesh.shape["col"])
    return jax.shard_map(
        functools.partial(body, *sizes), mesh=mesh, in_specs=in_specs, out_specs=out_specs, check_vma=False
    )
```

```python
import functools
import math

import jax
import jax.numpy as jnp
from jax import lax
from jax.experimental import pallas as pl
from jax.experimental.pallas import tpu as pltpu
from jax.sharding import PartitionSpec as P

gelu_coef = math.sqrt(2.0 / math.pi)
cubic_coef = 0.044715
MESH = pl.DeviceIdType.MESH
CHUNKS = 4


def gelu_parts(pre_f32):
    tangent = jnp.tanh(gelu_coef * (pre_f32 + cubic_coef * pre_f32 * pre_f32 * pre_f32))
    activated = 0.5 * pre_f32 * (1.0 + tangent)
    slopes = 0.5 * (1.0 + tangent) + 0.5 * pre_f32 * (1.0 - tangent * tangent) * gelu_coef * (
        1.0 + 3.0 * cubic_coef * pre_f32 * pre_f32
    )
    return (activated, slopes)


def contract(left_side, right_side, left_dim, right_dim):
    return lax.dot_general(
        left_side,
        right_side,
        (((left_dim,), (right_dim,)), ((), ())),
        preferred_element_type=jnp.float32,
    )


def exchange_kernel(
    n_row, n_col,
    tok_ref, grad_ref, pre_ref, w_ref, w_in_ref,
    tok_all, grad_all, act_all, pg_all, gt_ref,
    g_v, w_v, h_v, a_v, p_v, in_v, slope_v, wi_v, part_v, terms_v,
    w_sem, wi_sem, own_sem, out_sem, t_send, t_recv,
    g_send, g_recv, x_send, x_recv,
    h_send, h_recv, a_send, a_recv, p_send, p_recv,
):
    rows = grad_ref.shape[0]
    share = pre_ref.shape[0]
    width = w_v.shape[1]
    tile = 256 if width % 256 == 0 else 128
    last = n_col - 2
    row = lax.axis_index("row")
    col = lax.axis_index("col")
    odd = col % 2
    pos = (1 - odd) * (col // 2) + odd * (n_col - 1 - col // 2)

    def col_at(place):
        place = (place + 2 * n_col) % n_col
        back = place // (n_col // 2)
        return (1 - back) * (2 * place) + back * (2 * (n_col - 1 - place) + 1)

    def row_slice(index, size):
        return pl.ds(pl.multiple_of(index * size, size), size)

    def sign(q):
        return 1 if q % 2 == 0 else -1

    def ring(q, src, dst, send_sem, recv_sem):
        return pltpu.make_async_remote_copy(
            src_ref=src, dst_ref=dst, send_sem=send_sem, recv_sem=recv_sem,
            device_id=(row, col_at(pos + sign(q))), device_id_type=MESH,
        )

    def h_copy(q, step):
        return ring(q, in_v.at[q, step], in_v.at[q, step + 1], h_send.at[q, step + 1], h_recv.at[q, step + 1])

    def h_arrival(q, step):
        block = in_v.at[q, step]
        return ring(q, block, block, h_send.at[q, step], h_recv.at[q, step])

    def h_first(q):
        block = h_v.at[q, row_slice(col_at(pos - sign(q)), share)]
        return ring(q, block, in_v.at[q, 0], h_send.at[q, 0], h_recv.at[q, 0])

    def gather_copy(buf, send_sem, recv_sem, q, step):
        block = buf.at[q, row_slice(col_at(pos - sign(q) * step), share)]
        return ring(q, block, block, send_sem.at[q, step], recv_sem.at[q, step])

    def gather_arrival(buf, send_sem, recv_sem, q, step):
        block = buf.at[q, row_slice(col_at(pos - sign(q) * (step + 1)), share)]
        return ring(q, block, block, send_sem.at[q, step], recv_sem.at[q, step])

    a_ring = (a_v, a_send, a_recv)
    p_ring = (p_v, p_send, p_recv)

    w_loads = [
        pltpu.make_async_copy(w_ref.at[pl.ds(q * width, width)], w_v.at[q], w_sem.at[q])
        for q in range(CHUNKS)
    ]
    for load in w_loads:
        load.start()

    barrier = pltpu.get_barrier_semaphore()
    for k in range(1, n_row):
        pl.semaphore_signal(barrier, inc=1, device_id=((row + k) % n_row, col), device_id_type=MESH)
    for side in (1, -1):
        pl.semaphore_signal(barrier, inc=1, device_id=(row, col_at(pos + side)), device_id_type=MESH)
    pl.semaphore_wait(barrier, n_row + 1)

    def row_copy(src, dst, send_sem, recv_sem, k, owner):
        return pltpu.make_async_remote_copy(
            src_ref=src, dst_ref=dst.at[row_slice(owner, rows)],
            send_sem=send_sem.at[k - 1], recv_sem=recv_sem.at[k - 1],
            device_id=((row + k) % n_row, col), device_id_type=MESH,
        )

    pairs = n_row // 2
    sibling = row + 1 - 2 * (row % 2)

    def peer(m):
        return (row + 2 * m) % n_row

    def source_of(m):
        return (row + n_row - 2 * m) % n_row

    def grad_copy(index, src, owner, target):
        return pltpu.make_async_remote_copy(
            src_ref=src, dst_ref=g_v.at[row_slice(owner, rows)],
            send_sem=g_send.at[index], recv_sem=g_recv.at[index],
            device_id=(target, col), device_id_type=MESH,
        )

    def grad_arrival(index, owner):
        return grad_copy(index, grad_ref, owner, sibling)

    def grad_relay(m):
        owner = source_of(m)
        return grad_copy(pairs - 1 + m, g_v.at[row_slice(owner, rows)], owner, sibling)

    for m in range(1, pairs):
        grad_copy(m, grad_ref, row, peer(m)).start()
    grad_copy(0, grad_ref, row, sibling).start()
    g_v[row_slice(row, rows), :] = grad_ref[...]

    def forward_activated(step):
        for q in range(CHUNKS):
            gather_arrival(*a_ring, q, step).wait_recv()
            gather_copy(*a_ring, q, step + 1).start()

    for q in range(CHUNKS):
        @pl.loop(0, width // tile)
        def _(j, q=q):
            lanes = pl.ds(pl.multiple_of(j * tile, tile), tile)
            source = pl.ds(pl.multiple_of(q * width + j * tile, 128), tile)
            activated, slopes = gelu_parts(pre_ref[:, source].astype(jnp.float32))
            a_v[q, row_slice(col, share), lanes] = activated.astype(jnp.bfloat16)
            slope_v[q, :, lanes] = slopes

        gather_copy(*a_ring, q, 0).start()
        if q == 1:
            for m in range(1, pairs):
                grad_arrival(m, source_of(m)).wait_recv()
                grad_relay(m).start()

    grad_arrival(0, sibling).wait_recv()
    for m in range(1, pairs):
        grad_arrival(pairs - 1 + m, (sibling + n_row - 2 * m) % n_row).wait_recv()

    for q in range(CHUNKS):
        w_loads[q].wait()

        @pl.loop(0, width // tile)
        def _(j, q=q):
            lanes = pl.ds(pl.multiple_of(j * tile, tile), tile)
            h_v[q, :, lanes] = contract(g_v[...], w_v[q, lanes, :], 1, 1).astype(jnp.bfloat16)

        h_first(q).start()
        if q % 2 == 1:
            forward_activated(q // 2)

    wi_loads = [
        pltpu.make_async_copy(w_in_ref.at[:, pl.ds(q * width, width)], wi_v.at[q], wi_sem.at[q])
        for q in range(CHUNKS)
    ]
    for load in wi_loads:
        load.start()

    for k in range(1, n_row):
        row_copy(tok_ref, tok_all, x_send, x_recv, k, row).start()
    own_tokens = pltpu.make_async_copy(tok_ref, tok_all.at[row_slice(row, rows)], own_sem.at[0])
    own_tokens.start()
    grad_out = pltpu.make_async_copy(g_v, grad_all, own_sem.at[1])
    grad_out.start()

    def add_and_pass(q, step):
        h_arrival(q, step).wait_recv()
        own = h_v[q, row_slice(col_at(pos - sign(q) * (step + 2)), share), :]
        total = in_v[q, step].astype(jnp.float32) + own.astype(jnp.float32)
        in_v[q, step] = total.astype(jnp.bfloat16)
        h_copy(q, step).start()

    ahead = CHUNKS // 2

    @pl.loop(0, last - ahead)
    def _(step):
        for q in range(CHUNKS):
            add_and_pass(q, step)
            gather_arrival(*a_ring, q, step + ahead).wait_recv()
            gather_copy(*a_ring, q, step + ahead + 1).start()

    @pl.loop(last - ahead, last)
    def _(step):
        for q in range(CHUNKS):
            add_and_pass(q, step)

    for q in range(CHUNKS):
        h_arrival(q, last).wait_recv()
        mine = row_slice(col, share)
        total = in_v[q, last].astype(jnp.float32) + h_v[q, mine, :].astype(jnp.float32)
        p_v[q, mine, :] = (total * slope_v[q]).astype(jnp.bfloat16)
        gather_copy(*p_ring, q, 0).start()

    def write_out(buf, out, q, which):
        return pltpu.make_async_copy(
            buf.at[q], out.at[:, pl.ds(q * width, width)], out_sem.at[which, q]
        )

    for q in range(CHUNKS):
        gather_arrival(*a_ring, q, last).wait_recv()
        write_out(a_v, act_all, q, 0).start()

    @pl.loop(0, last)
    def _(step):
        for q in range(CHUNKS):
            gather_arrival(*p_ring, q, step).wait_recv()
            gather_copy(*p_ring, q, step + 1).start()

    for q in range(CHUNKS):
        gather_arrival(*p_ring, q, last).wait_recv()
        write_out(p_v, pg_all, q, 1).start()
        wi_loads[q].wait()

    def term_copy(j, k):
        target = (row + k) % n_row
        return pltpu.make_async_remote_copy(
            src_ref=part_v.at[j, row_slice(target, rows)], dst_ref=terms_v.at[j, k - 1],
            send_sem=t_send.at[j, k - 1], recv_sem=t_recv.at[j, k - 1],
            device_id=(target, col), device_id_type=MESH,
        )

    slabs, slab = part_v.shape[0], part_v.shape[2]
    for j in range(slabs):
        lines = pl.ds(j * slab, slab)
        total = contract(p_v[0], wi_v[0, lines, :], 1, 1)
        for q in range(1, CHUNKS):
            total = total + contract(p_v[q], wi_v[q, lines, :], 1, 1)
        part_v[j] = total.astype(jnp.bfloat16)
        for k in range(1, n_row):
            term_copy(j, k).start()

    for j in range(slabs):
        total = part_v[j, row_slice(row, rows), :].astype(jnp.float32)
        for k in range(1, n_row):
            term_copy(j, k).wait_recv()
            total = total + terms_v[j, k - 1].astype(jnp.float32)
        gt_ref[:, pl.ds(j * slab, slab)] = total.astype(jnp.bfloat16)

    for j in range(slabs):
        for k in range(1, n_row):
            term_copy(j, k).wait_send()
    grad_copy(0, grad_ref, row, sibling).wait_send()
    for m in range(1, pairs):
        grad_copy(m, grad_ref, row, peer(m)).wait_send()
        grad_relay(m).wait_send()
    for k in range(1, n_row):
        row_copy(tok_ref, tok_all, x_send, x_recv, k, row).wait_send()
        row_copy(tok_ref, tok_all, x_send, x_recv, k, (row + n_row - k) % n_row).wait_recv()
    own_tokens.wait()
    grad_out.wait()

    for q in range(CHUNKS):
        h_first(q).wait_send()

        @pl.loop(0, last)
        def _(step, q=q):
            h_copy(q, step).wait_send()

        @pl.loop(0, last + 1)
        def _(step, q=q):
            gather_copy(*a_ring, q, step).wait_send()
            gather_copy(*p_ring, q, step).wait_send()

        write_out(a_v, act_all, q, 0).wait()
        write_out(p_v, pg_all, q, 1).wait()


def weight_kernel(scale, tok_ref, grad_ref, act_ref, pg_ref, w_in_ref, w_out_ref, tok_t):
    @pl.when(pl.program_id(0) == 0)
    def _():
        tok_t[...] = tok_ref[...].T

    w_out_ref[...] = (contract(act_ref[...], grad_ref[...], 0, 0) * scale).astype(jnp.bfloat16)
    w_in_ref[...] = (contract(tok_t[...], pg_ref[...], 1, 0) * scale).astype(jnp.bfloat16)


def weight_grads(tok_all, grad_all, hid_all, pregrad_all):
    total, depth = tok_all.shape
    units = hid_all.shape[1]
    tile = 512 if units % 512 == 0 else 128
    scale = float(total) ** (-0.5)
    whole = pl.BlockSpec((total, depth), lambda i: (0, 0))
    columns = pl.BlockSpec((total, tile), lambda i: (0, i))
    return pl.pallas_call(
        functools.partial(weight_kernel, scale),
        grid=(units // tile,),
        out_shape=(
            jax.ShapeDtypeStruct((depth, units), jnp.bfloat16),
            jax.ShapeDtypeStruct((units, depth), jnp.bfloat16),
        ),
        in_specs=[whole, whole, columns, columns],
        out_specs=(
            pl.BlockSpec((depth, tile), lambda i: (0, i)),
            pl.BlockSpec((tile, depth), lambda i: (i, 0)),
        ),
        scratch_shapes=[pltpu.VMEM((depth, total), jnp.bfloat16)],
        compiler_params=pltpu.CompilerParams(vmem_limit_bytes=56 * 2**20),
        cost_estimate=pl.CostEstimate(
            flops=4 * total * depth * units,
            bytes_accessed=4 * units * (total + depth) + 4 * total * depth,
            transcendentals=0,
        ),
        name="weight_grads",
    )(tok_all, grad_all, hid_all, pregrad_all)


def body(n_row, n_col, tokens, out_grad, pre_act, w_in, w_out):
    rows, depth = tokens.shape
    share, units = pre_act.shape
    total = rows * n_row
    width = units // CHUNKS
    slab = 256 if depth % 256 == 0 else 128
    half = jnp.bfloat16
    dma = pltpu.SemaphoreType.DMA
    ring_sem = dma((CHUNKS, n_col - 1))
    row_sem = dma((n_row - 1,))
    vmem = pl.BlockSpec(memory_space=pltpu.VMEM)
    anywhere = pl.BlockSpec(memory_space=pl.ANY)
    tok_all, grad_all, hid_all, pregrad_all, grad_tokens = pl.pallas_call(
        functools.partial(exchange_kernel, n_row, n_col),
        out_shape=(
            jax.ShapeDtypeStruct((total, depth), half),
            jax.ShapeDtypeStruct((total, depth), half),
            jax.ShapeDtypeStruct((total, units), half),
            jax.ShapeDtypeStruct((total, units), half),
            jax.ShapeDtypeStruct((rows, depth), half),
        ),
        in_specs=[vmem, vmem, vmem, anywhere, anywhere],
        out_specs=(anywhere,) * 4 + (vmem,),
        scratch_shapes=[
            pltpu.VMEM((total, depth), half),
            pltpu.VMEM((CHUNKS, width, depth), half),
            pltpu.VMEM((CHUNKS, total, width), half),
            pltpu.VMEM((CHUNKS, total, width), half),
            pltpu.VMEM((CHUNKS, total, width), half),
            pltpu.VMEM((CHUNKS, n_col - 1, share, width), half),
            pltpu.VMEM((CHUNKS, share, width), jnp.float32),
            pltpu.VMEM((CHUNKS, depth, width), half),
            pltpu.VMEM((depth // slab, total, slab), half),
            pltpu.VMEM((depth // slab, n_row - 1, rows, slab), half),
            dma((CHUNKS,)), dma((CHUNKS,)), dma((2,)), dma((2, CHUNKS)),
            dma((depth // slab, n_row - 1)), dma((depth // slab, n_row - 1)),
            row_sem, row_sem, row_sem, row_sem,
            ring_sem, ring_sem, ring_sem, ring_sem, ring_sem, ring_sem,
        ],
        compiler_params=pltpu.CompilerParams(
            collective_id=0, has_side_effects=True, vmem_limit_bytes=58 * 2**20
        ),
        cost_estimate=pl.CostEstimate(
            flops=2 * total * depth * units, bytes_accessed=40 * 2**20, transcendentals=share * units
        ),
        name="exchange",
    )(tokens, out_grad, pre_act, w_out, w_in)
    grad_w_in, grad_w_out = weight_grads(tok_all, grad_all, hid_all, pregrad_all)
    return (grad_tokens, grad_w_in, grad_w_out)


def solution(mesh):
    in_specs = (P("row", "col"), P("row", "col"), P("col", "row"), P("col", "row"), P("row", "col"))
    out_specs = (P("row", "col"), P("col", "row"), P("row", "col"))
    sizes = (mesh.shape["row"], mesh.shape["col"])
    return jax.shard_map(
        functools.partial(body, *sizes), mesh=mesh, in_specs=in_specs, out_specs=out_specs, check_vma=False
    )
```

```python
import functools
import math

import jax
import jax.numpy as jnp
from jax import lax
from jax.experimental import pallas as pl
from jax.experimental.pallas import tpu as pltpu
from jax.sharding import PartitionSpec as P

gelu_coef = math.sqrt(2.0 / math.pi)
cubic_coef = 0.044715
MESH = pl.DeviceIdType.MESH
CHUNKS = 4


def gelu_parts(pre_f32):
    tangent = jnp.tanh(gelu_coef * (pre_f32 + cubic_coef * pre_f32 * pre_f32 * pre_f32))
    activated = 0.5 * pre_f32 * (1.0 + tangent)
    slopes = 0.5 * (1.0 + tangent) + 0.5 * pre_f32 * (1.0 - tangent * tangent) * gelu_coef * (
        1.0 + 3.0 * cubic_coef * pre_f32 * pre_f32
    )
    return (activated, slopes)


def contract(left_side, right_side, left_dim, right_dim):
    return lax.dot_general(
        left_side,
        right_side,
        (((left_dim,), (right_dim,)), ((), ())),
        preferred_element_type=jnp.float32,
    )


def exchange_kernel(
    n_row, n_col,
    tok_ref, grad_ref, pre_ref, w_ref, w_in_ref,
    tok_all, grad_all, act_all, pg_all, gt_ref,
    g_v, w_v, h_v, a_v, p_v, in_v, slope_v, wi_v, part_v, terms_v,
    w_sem, wi_sem, own_sem, out_sem, t_send, t_recv,
    g_send, g_recv, x_send, x_recv,
    h_send, h_recv, a_send, a_recv, p_send, p_recv,
):
    rows = grad_ref.shape[0]
    share = pre_ref.shape[0]
    width = w_v.shape[1]
    tile = 256 if width % 256 == 0 else 128
    last = n_col - 2
    row = lax.axis_index("row")
    col = lax.axis_index("col")
    odd = col % 2
    pos = (1 - odd) * (col // 2) + odd * (n_col - 1 - col // 2)

    def col_at(place):
        place = (place + 2 * n_col) % n_col
        back = place // (n_col // 2)
        return (1 - back) * (2 * place) + back * (2 * (n_col - 1 - place) + 1)

    def row_slice(index, size):
        return pl.ds(pl.multiple_of(index * size, size), size)

    def sign(q):
        return 1 if q % 2 == 0 else -1

    def ring(q, src, dst, send_sem, recv_sem):
        return pltpu.make_async_remote_copy(
            src_ref=src, dst_ref=dst, send_sem=send_sem, recv_sem=recv_sem,
            device_id=(row, col_at(pos + sign(q))), device_id_type=MESH,
        )

    def h_copy(q, step):
        return ring(q, in_v.at[q, step], in_v.at[q, step + 1], h_send.at[q, step + 1], h_recv.at[q, step + 1])

    def h_arrival(q, step):
        block = in_v.at[q, step]
        return ring(q, block, block, h_send.at[q, step], h_recv.at[q, step])

    def h_first(q):
        block = h_v.at[q, row_slice(col_at(pos - sign(q)), share)]
        return ring(q, block, in_v.at[q, 0], h_send.at[q, 0], h_recv.at[q, 0])

    def gather_copy(buf, send_sem, recv_sem, q, step):
        block = buf.at[q, row_slice(col_at(pos - sign(q) * step), share)]
        return ring(q, block, block, send_sem.at[q, step], recv_sem.at[q, step])

    def gather_arrival(buf, send_sem, recv_sem, q, step):
        block = buf.at[q, row_slice(col_at(pos - sign(q) * (step + 1)), share)]
        return ring(q, block, block, send_sem.at[q, step], recv_sem.at[q, step])

    a_ring = (a_v, a_send, a_recv)
    p_ring = (p_v, p_send, p_recv)

    w_loads = [
        pltpu.make_async_copy(w_ref.at[pl.ds(q * width, width)], w_v.at[q], w_sem.at[q])
        for q in range(CHUNKS)
    ]
    for load in w_loads:
        load.start()

    barrier = pltpu.get_barrier_semaphore()
    for k in range(1, n_row):
        pl.semaphore_signal(barrier, inc=1, device_id=((row + k) % n_row, col), device_id_type=MESH)
    for side in (1, -1):
        pl.semaphore_signal(barrier, inc=1, device_id=(row, col_at(pos + side)), device_id_type=MESH)
    pl.semaphore_wait(barrier, n_row + 1)

    def row_copy(src, dst, send_sem, recv_sem, k, owner):
        return pltpu.make_async_remote_copy(
            src_ref=src, dst_ref=dst.at[row_slice(owner, rows)],
            send_sem=send_sem.at[k - 1], recv_sem=recv_sem.at[k - 1],
            device_id=((row + k) % n_row, col), device_id_type=MESH,
        )

    pairs = n_row // 2
    sibling = row + 1 - 2 * (row % 2)

    def peer(m):
        return (row + 2 * m) % n_row

    def source_of(m):
        return (row + n_row - 2 * m) % n_row

    def grad_copy(index, src, owner, target):
        return pltpu.make_async_remote_copy(
            src_ref=src, dst_ref=g_v.at[row_slice(owner, rows)],
            send_sem=g_send.at[index], recv_sem=g_recv.at[index],
            device_id=(target, col), device_id_type=MESH,
        )

    def grad_arrival(index, owner):
        return grad_copy(index, grad_ref, owner, sibling)

    def grad_relay(m):
        owner = source_of(m)
        return grad_copy(pairs - 1 + m, g_v.at[row_slice(owner, rows)], owner, sibling)

    for m in range(1, pairs):
        grad_copy(m, grad_ref, row, peer(m)).start()
    grad_copy(0, grad_ref, row, sibling).start()
    g_v[row_slice(row, rows), :] = grad_ref[...]

    def forward_activated(step):
        for q in range(CHUNKS):
            gather_arrival(*a_ring, q, step).wait_recv()
            gather_copy(*a_ring, q, step + 1).start()

    for q in range(CHUNKS):
        @pl.loop(0, width // tile)
        def _(j, q=q):
            lanes = pl.ds(pl.multiple_of(j * tile, tile), tile)
            source = pl.ds(pl.multiple_of(q * width + j * tile, 128), tile)
            activated, slopes = gelu_parts(pre_ref[:, source].astype(jnp.float32))
            a_v[q, row_slice(col, share), lanes] = activated.astype(jnp.bfloat16)
            slope_v[q, :, lanes] = slopes

        gather_copy(*a_ring, q, 0).start()
        if q == 1:
            for m in range(1, pairs):
                grad_arrival(m, source_of(m)).wait_recv()
                grad_relay(m).start()

    grad_arrival(0, sibling).wait_recv()
    for m in range(1, pairs):
        grad_arrival(pairs - 1 + m, (sibling + n_row - 2 * m) % n_row).wait_recv()

    for q in range(CHUNKS):
        w_loads[q].wait()

        @pl.loop(0, width // tile)
        def _(j, q=q):
            lanes = pl.ds(pl.multiple_of(j * tile, tile), tile)
            h_v[q, :, lanes] = contract(g_v[...], w_v[q, lanes, :], 1, 1).astype(jnp.bfloat16)

        h_first(q).start()
        if q == 1:
            forward_activated(0)

    wi_loads = [
        pltpu.make_async_copy(w_in_ref.at[:, pl.ds(q * width, width)], wi_v.at[q], wi_sem.at[q])
        for q in range(CHUNKS)
    ]
    for load in wi_loads:
        load.start()

    for k in range(1, n_row):
        row_copy(tok_ref, tok_all, x_send, x_recv, k, row).start()
    own_tokens = pltpu.make_async_copy(tok_ref, tok_all.at[row_slice(row, rows)], own_sem.at[0])
    own_tokens.start()
    grad_out = pltpu.make_async_copy(g_v, grad_all, own_sem.at[1])
    grad_out.start()

    def add_and_pass(q, step):
        h_arrival(q, step).wait_recv()
        own = h_v[q, row_slice(col_at(pos - sign(q) * (step + 2)), share), :]
        total = in_v[q, step].astype(jnp.float32) + own.astype(jnp.float32)
        in_v[q, step] = total.astype(jnp.bfloat16)
        h_copy(q, step).start()

    @pl.loop(0, last // 2)
    def _(turn):
        for q in range(CHUNKS):
            add_and_pass(q, 2 * turn)
        forward_activated(turn + 1)
        for q in range(CHUNKS):
            add_and_pass(q, 2 * turn + 1)

    for q in range(CHUNKS):
        h_arrival(q, last).wait_recv()
        mine = row_slice(col, share)
        total = in_v[q, last].astype(jnp.float32) + h_v[q, mine, :].astype(jnp.float32)
        p_v[q, mine, :] = (total * slope_v[q]).astype(jnp.bfloat16)
        gather_copy(*p_ring, q, 0).start()

    def write_out(buf, out, q, which):
        return pltpu.make_async_copy(
            buf.at[q], out.at[:, pl.ds(q * width, width)], out_sem.at[which, q]
        )

    def forward_pre_grad(step):
        for q in range(CHUNKS):
            gather_arrival(*p_ring, q, step).wait_recv()
            gather_copy(*p_ring, q, step + 1).start()

    @pl.loop(0, last // 2 - 1)
    def _(turn):
        forward_pre_grad(2 * turn)
        forward_activated(last // 2 + 1 + turn)
        forward_pre_grad(2 * turn + 1)

    forward_pre_grad(last - 2)
    for q in range(CHUNKS):
        gather_arrival(*a_ring, q, last).wait_recv()
        write_out(a_v, act_all, q, 0).start()
    forward_pre_grad(last - 1)

    for q in range(CHUNKS):
        gather_arrival(*p_ring, q, last).wait_recv()
        write_out(p_v, pg_all, q, 1).start()
        wi_loads[q].wait()

    def term_copy(j, k):
        target = (row + k) % n_row
        return pltpu.make_async_remote_copy(
            src_ref=part_v.at[j, row_slice(target, rows)], dst_ref=terms_v.at[j, k - 1],
            send_sem=t_send.at[j, k - 1], recv_sem=t_recv.at[j, k - 1],
            device_id=(target, col), device_id_type=MESH,
        )

    slabs, slab = part_v.shape[0], part_v.shape[2]
    for j in range(slabs):
        lines = pl.ds(j * slab, slab)
        total = contract(p_v[0], wi_v[0, lines, :], 1, 1)
        for q in range(1, CHUNKS):
            total = total + contract(p_v[q], wi_v[q, lines, :], 1, 1)
        part_v[j] = total.astype(jnp.bfloat16)
        for k in range(1, n_row):
            term_copy(j, k).start()

    for j in range(slabs):
        total = part_v[j, row_slice(row, rows), :].astype(jnp.float32)
        for k in range(1, n_row):
            term_copy(j, k).wait_recv()
            total = total + terms_v[j, k - 1].astype(jnp.float32)
        gt_ref[:, pl.ds(j * slab, slab)] = total.astype(jnp.bfloat16)

    for j in range(slabs):
        for k in range(1, n_row):
            term_copy(j, k).wait_send()
    grad_copy(0, grad_ref, row, sibling).wait_send()
    for m in range(1, pairs):
        grad_copy(m, grad_ref, row, peer(m)).wait_send()
        grad_relay(m).wait_send()
    for k in range(1, n_row):
        row_copy(tok_ref, tok_all, x_send, x_recv, k, row).wait_send()
        row_copy(tok_ref, tok_all, x_send, x_recv, k, (row + n_row - k) % n_row).wait_recv()
    own_tokens.wait()
    grad_out.wait()

    for q in range(CHUNKS):
        h_first(q).wait_send()

        @pl.loop(0, last)
        def _(step, q=q):
            h_copy(q, step).wait_send()

        @pl.loop(0, last + 1)
        def _(step, q=q):
            gather_copy(*a_ring, q, step).wait_send()
            gather_copy(*p_ring, q, step).wait_send()

        write_out(a_v, act_all, q, 0).wait()
        write_out(p_v, pg_all, q, 1).wait()


def body(n_row, n_col, tokens, out_grad, pre_act, w_in, w_out):
    rows, depth = tokens.shape
    share, units = pre_act.shape
    total = rows * n_row
    width = units // CHUNKS
    slab = 256 if depth % 256 == 0 else 128
    half = jnp.bfloat16
    dma = pltpu.SemaphoreType.DMA
    ring_sem = dma((CHUNKS, n_col - 1))
    row_sem = dma((n_row - 1,))
    vmem = pl.BlockSpec(memory_space=pltpu.VMEM)
    anywhere = pl.BlockSpec(memory_space=pl.ANY)
    tok_all, grad_all, hid_all, pregrad_all, grad_tokens = pl.pallas_call(
        functools.partial(exchange_kernel, n_row, n_col),
        out_shape=(
            jax.ShapeDtypeStruct((total, depth), half),
            jax.ShapeDtypeStruct((total, depth), half),
            jax.ShapeDtypeStruct((total, units), half),
            jax.ShapeDtypeStruct((total, units), half),
            jax.ShapeDtypeStruct((rows, depth), half),
        ),
        in_specs=[vmem, vmem, vmem, anywhere, anywhere],
        out_specs=(anywhere,) * 4 + (vmem,),
        scratch_shapes=[
            pltpu.VMEM((total, depth), half),
            pltpu.VMEM((CHUNKS, width, depth), half),
            pltpu.VMEM((CHUNKS, total, width), half),
            pltpu.VMEM((CHUNKS, total, width), half),
            pltpu.VMEM((CHUNKS, total, width), half),
            pltpu.VMEM((CHUNKS, n_col - 1, share, width), half),
            pltpu.VMEM((CHUNKS, share, width), jnp.float32),
            pltpu.VMEM((CHUNKS, depth, width), half),
            pltpu.VMEM((depth // slab, total, slab), half),
            pltpu.VMEM((depth // slab, n_row - 1, rows, slab), half),
            dma((CHUNKS,)), dma((CHUNKS,)), dma((2,)), dma((2, CHUNKS)),
            dma((depth // slab, n_row - 1)), dma((depth // slab, n_row - 1)),
            row_sem, row_sem, row_sem, row_sem,
            ring_sem, ring_sem, ring_sem, ring_sem, ring_sem, ring_sem,
        ],
        compiler_params=pltpu.CompilerParams(
            collective_id=0, has_side_effects=True, vmem_limit_bytes=58 * 2**20
        ),
        cost_estimate=pl.CostEstimate(
            flops=2 * total * depth * units, bytes_accessed=40 * 2**20, transcendentals=share * units
        ),
        name="exchange",
    )(tokens, out_grad, pre_act, w_out, w_in)
    grad_scale = float(total) ** (-0.5)
    grad_w_out = (contract(hid_all, grad_all, 0, 0) * grad_scale).astype(half)
    grad_w_in = (contract(tok_all, pregrad_all, 0, 0) * grad_scale).astype(half)
    return (grad_tokens, grad_w_in, grad_w_out)


def solution(mesh):
    in_specs = (P("row", "col"), P("row", "col"), P("col", "row"), P("col", "row"), P("row", "col"))
    out_specs = (P("row", "col"), P("col", "row"), P("row", "col"))
    sizes = (mesh.shape["row"], mesh.shape["col"])
    return jax.shard_map(
        functools.partial(body, *sizes), mesh=mesh, in_specs=in_specs, out_specs=out_specs, check_vma=False
    )
```

```python
import functools
import math

import jax
import jax.numpy as jnp
from jax import lax
from jax.experimental import pallas as pl
from jax.experimental.pallas import tpu as pltpu
from jax.sharding import PartitionSpec as P

gelu_coef = math.sqrt(2.0 / math.pi)
cubic_coef = 0.044715
MESH = pl.DeviceIdType.MESH
CHUNKS = 4


def gelu_parts(pre_f32):
    tangent = jnp.tanh(gelu_coef * (pre_f32 + cubic_coef * pre_f32 * pre_f32 * pre_f32))
    activated = 0.5 * pre_f32 * (1.0 + tangent)
    slopes = 0.5 * (1.0 + tangent) + 0.5 * pre_f32 * (1.0 - tangent * tangent) * gelu_coef * (
        1.0 + 3.0 * cubic_coef * pre_f32 * pre_f32
    )
    return (activated, slopes)


def contract(left_side, right_side, left_dim, right_dim):
    return lax.dot_general(
        left_side,
        right_side,
        (((left_dim,), (right_dim,)), ((), ())),
        preferred_element_type=jnp.float32,
    )


def exchange_kernel(
    n_row, n_col,
    tok_ref, grad_ref, pre_ref, w_ref, w_in_ref,
    tok_all, grad_all, act_all, pg_all, gt_ref,
    g_v, w_v, h_v, a_v, p_v, in_v, slope_v, wi_v, part_v, terms_v, acc_v,
    w_sem, wi_sem, own_sem, out_sem, t_send, t_recv,
    g_send, g_recv, x_send, x_recv,
    h_send, h_recv, a_send, a_recv, p_send, p_recv,
):
    rows = grad_ref.shape[0]
    share = pre_ref.shape[0]
    width = w_v.shape[1]
    tile = 256 if width % 256 == 0 else 128
    last = n_col - 2
    row = lax.axis_index("row")
    col = lax.axis_index("col")
    odd = col % 2
    pos = (1 - odd) * (col // 2) + odd * (n_col - 1 - col // 2)

    def col_at(place):
        place = (place + 2 * n_col) % n_col
        back = place // (n_col // 2)
        return (1 - back) * (2 * place) + back * (2 * (n_col - 1 - place) + 1)

    def row_slice(index, size):
        return pl.ds(pl.multiple_of(index * size, size), size)

    def sign(q):
        return 1 if q % 2 == 0 else -1

    def ring(q, src, dst, send_sem, recv_sem):
        return pltpu.make_async_remote_copy(
            src_ref=src, dst_ref=dst, send_sem=send_sem, recv_sem=recv_sem,
            device_id=(row, col_at(pos + sign(q))), device_id_type=MESH,
        )

    def h_copy(q, step):
        return ring(q, in_v.at[q, step], in_v.at[q, step + 1], h_send.at[q, step + 1], h_recv.at[q, step + 1])

    def h_arrival(q, step):
        block = in_v.at[q, step]
        return ring(q, block, block, h_send.at[q, step], h_recv.at[q, step])

    def h_first(q):
        block = h_v.at[q, row_slice(col_at(pos - sign(q)), share)]
        return ring(q, block, in_v.at[q, 0], h_send.at[q, 0], h_recv.at[q, 0])

    def gather_copy(buf, send_sem, recv_sem, q, step):
        block = buf.at[q, row_slice(col_at(pos - sign(q) * step), share)]
        return ring(q, block, block, send_sem.at[q, step], recv_sem.at[q, step])

    def gather_arrival(buf, send_sem, recv_sem, q, step):
        block = buf.at[q, row_slice(col_at(pos - sign(q) * (step + 1)), share)]
        return ring(q, block, block, send_sem.at[q, step], recv_sem.at[q, step])

    a_ring = (a_v, a_send, a_recv)
    p_ring = (p_v, p_send, p_recv)

    w_loads = [
        pltpu.make_async_copy(w_ref.at[pl.ds(q * width, width)], w_v.at[q], w_sem.at[q])
        for q in range(CHUNKS)
    ]
    for load in w_loads:
        load.start()

    barrier = pltpu.get_barrier_semaphore()
    for k in range(1, n_row):
        pl.semaphore_signal(barrier, inc=1, device_id=((row + k) % n_row, col), device_id_type=MESH)
    for side in (1, -1):
        pl.semaphore_signal(barrier, inc=1, device_id=(row, col_at(pos + side)), device_id_type=MESH)
    pl.semaphore_wait(barrier, n_row + 1)

    def row_copy(src, dst, send_sem, recv_sem, k, owner):
        return pltpu.make_async_remote_copy(
            src_ref=src, dst_ref=dst.at[row_slice(owner, rows)],
            send_sem=send_sem.at[k - 1], recv_sem=recv_sem.at[k - 1],
            device_id=((row + k) % n_row, col), device_id_type=MESH,
        )

    pairs = n_row // 2
    sibling = row + 1 - 2 * (row % 2)

    def peer(m):
        return (row + 2 * m) % n_row

    def source_of(m):
        return (row + n_row - 2 * m) % n_row

    def grad_copy(index, src, owner, target):
        return pltpu.make_async_remote_copy(
            src_ref=src, dst_ref=g_v.at[row_slice(owner, rows)],
            send_sem=g_send.at[index], recv_sem=g_recv.at[index],
            device_id=(target, col), device_id_type=MESH,
        )

    def grad_arrival(index, owner):
        return grad_copy(index, grad_ref, owner, sibling)

    def grad_relay(m):
        owner = source_of(m)
        return grad_copy(pairs - 1 + m, g_v.at[row_slice(owner, rows)], owner, sibling)

    for m in range(1, pairs):
        grad_copy(m, grad_ref, row, peer(m)).start()
    grad_copy(0, grad_ref, row, sibling).start()
    g_v[row_slice(row, rows), :] = grad_ref[...]

    def forward_activated(step):
        for q in range(CHUNKS):
            gather_arrival(*a_ring, q, step).wait_recv()
            gather_copy(*a_ring, q, step + 1).start()

    for q in range(CHUNKS):
        @pl.loop(0, width // tile)
        def _(j, q=q):
            lanes = pl.ds(pl.multiple_of(j * tile, tile), tile)
            source = pl.ds(pl.multiple_of(q * width + j * tile, 128), tile)
            activated, slopes = gelu_parts(pre_ref[:, source].astype(jnp.float32))
            a_v[q, row_slice(col, share), lanes] = activated.astype(jnp.bfloat16)
            slope_v[q, :, lanes] = slopes

        gather_copy(*a_ring, q, 0).start()
        if q == 1:
            for m in range(1, pairs):
                grad_arrival(m, source_of(m)).wait_recv()
                grad_relay(m).start()

    grad_arrival(0, sibling).wait_recv()
    for m in range(1, pairs):
        grad_arrival(pairs - 1 + m, (sibling + n_row - 2 * m) % n_row).wait_recv()

    for q in range(CHUNKS):
        w_loads[q].wait()

        @pl.loop(0, width // tile)
        def _(j, q=q):
            lanes = pl.ds(pl.multiple_of(j * tile, tile), tile)
            h_v[q, :, lanes] = contract(g_v[...], w_v[q, lanes, :], 1, 1).astype(jnp.bfloat16)

        h_first(q).start()
        if q == 1:
            forward_activated(0)

    wi_loads = [
        pltpu.make_async_copy(w_in_ref.at[:, pl.ds(q * width, width)], wi_v.at[q], wi_sem.at[q])
        for q in range(CHUNKS)
    ]
    for load in wi_loads:
        load.start()

    for k in range(1, n_row):
        row_copy(tok_ref, tok_all, x_send, x_recv, k, row).start()
    own_tokens = pltpu.make_async_copy(tok_ref, tok_all.at[row_slice(row, rows)], own_sem.at[0])
    own_tokens.start()
    grad_out = pltpu.make_async_copy(g_v, grad_all, own_sem.at[1])
    grad_out.start()

    def add_and_pass(q, step):
        h_arrival(q, step).wait_recv()
        own = h_v[q, row_slice(col_at(pos - sign(q) * (step + 2)), share), :]
        total = in_v[q, step].astype(jnp.float32) + own.astype(jnp.float32)
        in_v[q, step] = total.astype(jnp.bfloat16)
        h_copy(q, step).start()

    @pl.loop(0, last // 2)
    def _(turn):
        for q in range(CHUNKS):
            add_and_pass(q, 2 * turn)
        forward_activated(turn + 1)
        for q in range(CHUNKS):
            add_and_pass(q, 2 * turn + 1)

    for q in range(CHUNKS):
        h_arrival(q, last).wait_recv()
        mine = row_slice(col, share)
        total = in_v[q, last].astype(jnp.float32) + h_v[q, mine, :].astype(jnp.float32)
        p_v[q, mine, :] = (total * slope_v[q]).astype(jnp.bfloat16)
        gather_copy(*p_ring, q, 0).start()

    def write_out(buf, out, q, which):
        return pltpu.make_async_copy(
            buf.at[q], out.at[:, pl.ds(q * width, width)], out_sem.at[which, q]
        )

    def forward_pre_grad(step):
        for q in range(CHUNKS):
            gather_arrival(*p_ring, q, step).wait_recv()
            gather_copy(*p_ring, q, step + 1).start()

    @pl.loop(0, last // 2 - 1)
    def _(turn):
        forward_pre_grad(2 * turn)
        forward_activated(last // 2 + 1 + turn)
        forward_pre_grad(2 * turn + 1)

    forward_pre_grad(last - 2)
    for q in range(CHUNKS):
        gather_arrival(*a_ring, q, last).wait_recv()
        write_out(a_v, act_all, q, 0).start()
    forward_pre_grad(last - 1)

    for q in range(CHUNKS):
        gather_arrival(*p_ring, q, last).wait_recv()
        write_out(p_v, pg_all, q, 1).start()
        wi_loads[q].wait()
        if q < CHUNKS - 1:
            for j in range(part_v.shape[0]):
                piece = contract(p_v[q], wi_v[q, pl.ds(j * part_v.shape[2], part_v.shape[2]), :], 1, 1)
                acc_v[j] = piece if q == 0 else acc_v[j] + piece

    def term_copy(j, k):
        target = (row + k) % n_row
        return pltpu.make_async_remote_copy(
            src_ref=part_v.at[j, row_slice(target, rows)], dst_ref=terms_v.at[j, k - 1],
            send_sem=t_send.at[j, k - 1], recv_sem=t_recv.at[j, k - 1],
            device_id=(target, col), device_id_type=MESH,
        )

    slabs, slab = part_v.shape[0], part_v.shape[2]
    for j in range(slabs):
        lines = pl.ds(j * slab, slab)
        total = acc_v[j] + contract(p_v[CHUNKS - 1], wi_v[CHUNKS - 1, lines, :], 1, 1)
        part_v[j] = total.astype(jnp.bfloat16)
        for k in range(1, n_row):
            term_copy(j, k).start()

    for j in range(slabs):
        total = part_v[j, row_slice(row, rows), :].astype(jnp.float32)
        for k in range(1, n_row):
            term_copy(j, k).wait_recv()
            total = total + terms_v[j, k - 1].astype(jnp.float32)
        gt_ref[:, pl.ds(j * slab, slab)] = total.astype(jnp.bfloat16)

    for j in range(slabs):
        for k in range(1, n_row):
            term_copy(j, k).wait_send()
    grad_copy(0, grad_ref, row, sibling).wait_send()
    for m in range(1, pairs):
        grad_copy(m, grad_ref, row, peer(m)).wait_send()
        grad_relay(m).wait_send()
    for k in range(1, n_row):
        row_copy(tok_ref, tok_all, x_send, x_recv, k, row).wait_send()
        row_copy(tok_ref, tok_all, x_send, x_recv, k, (row + n_row - k) % n_row).wait_recv()
    own_tokens.wait()
    grad_out.wait()

    for q in range(CHUNKS):
        h_first(q).wait_send()

        @pl.loop(0, last)
        def _(step, q=q):
            h_copy(q, step).wait_send()

        @pl.loop(0, last + 1)
        def _(step, q=q):
            gather_copy(*a_ring, q, step).wait_send()
            gather_copy(*p_ring, q, step).wait_send()

        write_out(a_v, act_all, q, 0).wait()
        write_out(p_v, pg_all, q, 1).wait()


def body(n_row, n_col, tokens, out_grad, pre_act, w_in, w_out):
    rows, depth = tokens.shape
    share, units = pre_act.shape
    total = rows * n_row
    width = units // CHUNKS
    slab = 256 if depth % 256 == 0 else 128
    half = jnp.bfloat16
    dma = pltpu.SemaphoreType.DMA
    ring_sem = dma((CHUNKS, n_col - 1))
    row_sem = dma((n_row - 1,))
    vmem = pl.BlockSpec(memory_space=pltpu.VMEM)
    anywhere = pl.BlockSpec(memory_space=pl.ANY)
    tok_all, grad_all, hid_all, pregrad_all, grad_tokens = pl.pallas_call(
        functools.partial(exchange_kernel, n_row, n_col),
        out_shape=(
            jax.ShapeDtypeStruct((total, depth), half),
            jax.ShapeDtypeStruct((total, depth), half),
            jax.ShapeDtypeStruct((total, units), half),
            jax.ShapeDtypeStruct((total, units), half),
            jax.ShapeDtypeStruct((rows, depth), half),
        ),
        in_specs=[vmem, vmem, vmem, anywhere, anywhere],
        out_specs=(anywhere,) * 4 + (vmem,),
        scratch_shapes=[
            pltpu.VMEM((total, depth), half),
            pltpu.VMEM((CHUNKS, width, depth), half),
            pltpu.VMEM((CHUNKS, total, width), half),
            pltpu.VMEM((CHUNKS, total, width), half),
            pltpu.VMEM((CHUNKS, total, width), half),
            pltpu.VMEM((CHUNKS, n_col - 1, share, width), half),
            pltpu.VMEM((CHUNKS, share, width), jnp.float32),
            pltpu.VMEM((CHUNKS, depth, width), half),
            pltpu.VMEM((depth // slab, total, slab), half),
            pltpu.VMEM((depth // slab, n_row - 1, rows, slab), half),
            pltpu.VMEM((depth // slab, total, slab), jnp.float32),
            dma((CHUNKS,)), dma((CHUNKS,)), dma((2,)), dma((2, CHUNKS)),
            dma((depth // slab, n_row - 1)), dma((depth // slab, n_row - 1)),
            row_sem, row_sem, row_sem, row_sem,
            ring_sem, ring_sem, ring_sem, ring_sem, ring_sem, ring_sem,
        ],
        compiler_params=pltpu.CompilerParams(
            collective_id=0, has_side_effects=True, vmem_limit_bytes=58 * 2**20
        ),
        cost_estimate=pl.CostEstimate(
            flops=2 * total * depth * units, bytes_accessed=40 * 2**20, transcendentals=share * units
        ),
        name="exchange",
    )(tokens, out_grad, pre_act, w_out, w_in)
    grad_scale = float(total) ** (-0.5)
    grad_w_out = (contract(hid_all, grad_all, 0, 0) * grad_scale).astype(half)
    grad_w_in = (contract(tok_all, pregrad_all, 0, 0) * grad_scale).astype(half)
    return (grad_tokens, grad_w_in, grad_w_out)


def solution(mesh):
    in_specs = (P("row", "col"), P("row", "col"), P("col", "row"), P("col", "row"), P("row", "col"))
    out_specs = (P("row", "col"), P("col", "row"), P("row", "col"))
    sizes = (mesh.shape["row"], mesh.shape["col"])
    return jax.shard_map(
        functools.partial(body, *sizes), mesh=mesh, in_specs=in_specs, out_specs=out_specs, check_vma=False
    )
```
